32 devices in a mesh: groups: 2 (over x), row: 8 (over z, y), col: 2 (over core).
Axes of the slice: x: 2, y: 2, z: 4, core: 2. Of those that a mesh axis runs over, the one named last changes fastest.
Arguments:
- points: float32 [32768, 128], P(('groups', 'row', 'col')), parts along dimension 0, may hold values from -8 to 8, as said below
- start: float32 [32768, 64], P(('groups', 'row', 'col')), parts along dimension 0, may hold values from -6 to 6
- pair_mask: int32 [32, 7], P(('groups', 'row', 'col')), parts along dimension 0, may hold values from 0 to 1, as said below
Outputs:
- embedding: float32 [32768, 64], P(('groups', 'row', 'col')), parts along dimension 0
- degree: float32 [32768], P(('groups', 'row', 'col')), parts along dimension 0
The draws below stay inside these ranges and needn't reach their ends.
There are 2 independent parts, one for each index of `groups`. The reference program is written for one: setup_inputs(seed, part) draws one part's arguments, and reference() takes and returns one part's arrays. A program takes and returns all parts, laid end to end along the dimension named above; each array names one. Nothing has to cross between parts.
Inputs may be any that keep to these rules, and one draw needn't show every extreme that they name: pair_mask[b, d - 1] is 1 where block b pairs with block b + d, and 0 wherever b + d >= 16; blocks differ in how many partners they have. `points`: independent features of order one.
All inputs are finite; a program needn't handle non-finite values.
Results may differ from the reference program's by a relative error of at most 0.0042.
Values may be sent and summed in bfloat16 or wider, within the bound.
A program may use at most 64 MiB of HBM per device.

```python
import jax
import jax.numpy as jnp
from jax import lax

F = 128
K = 64
BLK = 1024
SPAN = 7
STEPS = 2
NBLK = 16
NPTS = 16384


def draw_points(key, part):
    key = jax.random.fold_in(key, 11)
    values = jnp.clip(jax.random.normal(key, (NPTS, F), jnp.float32), -6.0, 6.0)
    return values


def draw_pair_mask(key, part):
    key = jax.random.fold_in(key, 23)
    level_key, roll_key = jax.random.split(key)
    levels = jax.random.randint(level_key, (NBLK, 1), 1, 6)
    rolls = jax.random.randint(roll_key, (NBLK, SPAN), 0, 5)
    reach = jnp.arange(NBLK, dtype=jnp.int32)[:, None] + jnp.arange(1, SPAN + 1, dtype=jnp.int32)[None, :]
    inside = (reach < NBLK).astype(jnp.int32)
    return (rolls < levels).astype(jnp.int32) * inside


def block_scale(key, shape, cuts, smallest, high):
    loudness, own = 1.0, jax.random.fold_in(key, 6)
    for position, shards_of in cuts:
        draws = jnp.exp(jax.random.uniform(jax.random.fold_in(own, position), (shards_of,), jnp.float32, smallest / len(cuts), high / len(cuts)))
        loudness = loudness * jnp.repeat(draws, shape[position] // shards_of).reshape([-1 if axis == position else 1 for axis in range(len(shape))])
    return loudness


def noise(rng, extent, spread, most, cuts=(), kind=jnp.bfloat16):
    array = spread * jax.random.normal(rng, extent, jnp.float32)
    if cuts:
        array = array * block_scale(rng, extent, cuts, -0.22, 0.18)
    return jnp.clip(array, -most, most).astype(kind)


def setup_inputs(seed: int = 0, part: int = 0) -> dict:
    arg_keys = jax.random.split(jax.random.key(seed), 4)
    part_keys = jax.random.split(jax.random.fold_in(arg_keys[3], part), 4)
    points = draw_points(jax.random.fold_in(jax.random.fold_in(arg_keys[3], part), 71), part)
    start = noise(part_keys[1], (NPTS, K), 1.0, 6.0, ((0, 16),), jnp.float32)
    pair_mask = draw_pair_mask(jax.random.fold_in(jax.random.fold_in(arg_keys[3], part), 71), part)
    return dict(points=points, start=start, pair_mask=pair_mask)


def affinity_tile(near_rows, far_rows, weight_on):
    near_sq = lax.optimization_barrier(jnp.sum(near_rows * near_rows, axis=1))
    far_sq = lax.optimization_barrier(jnp.sum(far_rows * far_rows, axis=1))
    inner_prod = jnp.dot(near_rows.astype(jnp.float32), far_rows.T.astype(jnp.float32), precision=lax.Precision.HIGHEST, preferred_element_type=jnp.float32)
    distance = near_sq[:, None] + far_sq[None, :] - 2.0 * inner_prod
    return (jnp.exp(-(4.0 / near_rows.shape[1]) * distance) * weight_on).astype(jnp.bfloat16)

def spread_back(column_parts):
    summed = jnp.zeros(column_parts.shape[1:], jnp.float32)
    for offset in range(1, SPAN + 1):
        moved = jnp.concatenate([jnp.zeros((offset,) + column_parts.shape[2:], jnp.float32), column_parts[offset - 1, :NBLK - offset]], 0)
        summed = summed + moved
    return summed

def reference(points, start, pair_mask):
    blocks = points.reshape(NBLK, BLK, F)
    padded = jnp.concatenate([blocks, jnp.zeros((SPAN, BLK, F), jnp.float32)], 0)
    block_ids = jnp.arange(NBLK, dtype=jnp.int32)
    reach = block_ids[:, None] + jnp.arange(1, SPAN + 1, dtype=jnp.int32)[None, :]
    weights_on = jnp.concatenate([jnp.ones((NBLK, 1), jnp.float32), (pair_mask * (reach < NBLK).astype(jnp.int32)).astype(jnp.float32)], 1)

    def tile_of(block, offset):
        far_rows = lax.dynamic_slice_in_dim(padded, (block + offset).astype(jnp.int32), 1, 0)[0]
        return affinity_tile(blocks[block], far_rows, weights_on[block, offset])

    def degree_block(block):
        row_sums = jnp.zeros((BLK,), jnp.float32)
        column_sums = []
        for offset in range(SPAN + 1):
            affinity = tile_of(block, offset).astype(jnp.float32)
            row_sums = row_sums + lax.optimization_barrier(jnp.sum(affinity, axis=1))
            if offset > 0:
                column_sums.append(lax.optimization_barrier(jnp.sum(affinity, axis=0)))
        return (row_sums, jnp.stack(column_sums, 0))
    row_sums, column_sums = lax.map(degree_block, block_ids)
    degree = row_sums + spread_back(jnp.transpose(column_sums, (1, 0, 2)))
    inverse_root = lax.rsqrt(degree)
    current = start.reshape(NBLK, BLK, K)
    for iteration in range(STEPS):
        embedded = (inverse_root[:, :, None] * current).astype(jnp.bfloat16)
        embed_pad = jnp.concatenate([embedded, jnp.zeros((SPAN, BLK, K), jnp.bfloat16)], 0)

        def product_block(block):
            forward = jnp.zeros((BLK, K), jnp.float32)
            returns = []
            for offset in range(SPAN + 1):
                affinity = tile_of(block, offset).astype(jnp.float32)
                far_embed = lax.dynamic_slice_in_dim(embed_pad, (block + offset).astype(jnp.int32), 1, 0)[0].astype(jnp.float32)
                forward = forward + jnp.dot(affinity.astype(jnp.float32), far_embed.astype(jnp.float32), preferred_element_type=jnp.float32)
                if offset > 0:
                    returns.append(jnp.dot(affinity.T.astype(jnp.float32), embedded[block].astype(jnp.float32), preferred_element_type=jnp.float32))
            return (forward, jnp.stack(returns, 0))
        forward, returns = lax.map(product_block, block_ids)
        summed = forward + spread_back(jnp.transpose(returns, (1, 0, 2, 3)))
        y_rows = (inverse_root[:, :, None] * summed).reshape(NPTS, K)
        gram_matrix = jnp.dot(y_rows.T.astype(jnp.float32), y_rows.astype(jnp.float32), precision=lax.Precision.HIGHEST, preferred_element_type=jnp.float32) / NPTS
        factor = jnp.linalg.cholesky(gram_matrix)
        solved = lax.linalg.triangular_solve(factor, y_rows, left_side=False, lower=True, transpose_a=True)
        current = solved.reshape(NBLK, BLK, K)
    return (current.reshape(NPTS, K), degree.reshape(NPTS))
```

```python
import functools
import math

import jax
import jax.numpy as jnp
from jax import lax
from jax.experimental import pallas as pl
from jax.experimental.pallas import tpu as pltpu
from jax.sharding import PartitionSpec as P

STEPS = 2
MESH = pl.DeviceIdType.MESH
PAD = 16


def inverse_cholesky(gram):
    n = gram.shape[0]
    rows = lax.broadcasted_iota(jnp.int32, (n, 2 * n), 0)
    lanes = lax.broadcasted_iota(jnp.int32, (n, 2 * n), 1)
    eye = jnp.where(lanes == rows + n, 1.0, 0.0)
    mat = jnp.concatenate([gram, jnp.zeros_like(gram)], axis=1) + eye
    diag = jnp.ones((n, 1), jnp.float32)
    row_of = lax.broadcasted_iota(jnp.int32, (n, 1), 0)
    for k in range(n):
        pivot = mat[k:k + 1, k:k + 1]
        diag = jnp.where(row_of == k, pivot, diag)
        if k < n - 1:
            line = mat[k:k + 1, :] * (1.0 / pivot)
            column = jnp.where(row_of > k, mat[:, k:k + 1], 0.0)
            mat = mat - column * line
    return mat[:, n:] * lax.rsqrt(diag)


def kernel(rows_n, span, points_ref, start_ref, mask_ref, out_ref, degree_ref,
           pts, near_t, tiles, emb, acc, y_t, gram, gram_near, gram_all, gram_sum,
           pts_send, pts_recv, emb_send, emb_recv, gsend, grecv, gall_send, gall_recv):
    group = lax.axis_index("groups")
    chip = lax.axis_index("row")
    core = lax.axis_index("col")
    mine = 2 * chip + core
    total = 2 * rows_n
    other = 1 - core
    side = 1 - 2 * core
    blk = points_ref.shape[0]
    width = start_ref.shape[1]
    feats = points_ref.shape[1]
    reach = span // 2
    c2 = 4.0 / feats * math.log2(math.e)

    far_chip = chip + (reach + 1) * (2 * core - 1)
    has_far = jnp.logical_and(far_chip >= 0, far_chip < rows_n)

    barrier = pltpu.get_barrier_semaphore()

    def greet(o, _):
        pl.semaphore_signal(barrier, inc=1, device_id=(group, lax.rem(chip + o, rows_n), core), device_id_type=MESH)
        return 0

    lax.fori_loop(1, rows_n, greet, 0)
    pl.semaphore_signal(barrier, inc=1, device_id=(group, chip, other), device_id_type=MESH)

    @pl.when(has_far)
    def _():
        pl.semaphore_signal(barrier, inc=1, device_id=(group, far_chip, other), device_id_type=MESH)

    pts[span, 0:blk, :] = points_ref[...].astype(jnp.bfloat16)
    lane = lax.broadcasted_iota(jnp.int32, (PAD, feats), 1)
    flags = jnp.where(lane == feats - 1, 1.0, 0.0)
    for i in range(span):
        flags = jnp.where(lane == i, mask_ref[0, i].astype(jnp.float32), flags)
    pts[span, blk:blk + PAD, :] = flags.astype(jnp.bfloat16)

    pl.semaphore_wait(barrier, rows_n + has_far.astype(jnp.int32))

    def send_to(buf, send, recv, from_slot, to_slot, sem, to_chip, to_core):
        return pltpu.make_async_remote_copy(
            src_ref=buf.at[from_slot], dst_ref=buf.at[to_slot],
            send_sem=send.at[sem], recv_sem=recv.at[to_slot],
            device_id=(group, to_chip, to_core), device_id_type=MESH)

    def own_sends(buf, send, recv, action):
        def near(apart):
            @pl.when(jnp.logical_and(chip + apart >= 0, chip + apart < rows_n))
            def _():
                action(send_to(buf, send, recv, span, span - 2 * apart, span + 2 * apart, chip + apart, core))

        action(send_to(buf, send, recv, span, span - side, span, chip, other))
        for apart in range(1, reach + 1):
            near(apart)
            near(-apart)

        @pl.when(has_far)
        def _():
            action(send_to(buf, send, recv, span, span - span * (2 * core - 1), 2 * span + 1, far_chip, other))

    def relay(buf, send, recv, d):
        return send_to(buf, send, recv, span + d, span + d - side, span + d + 1, chip, other)

    def exchange(buf, send, recv, use):
        own_sends(buf, send, recv, lambda copy: copy.start())

        def turn(t, _):
            g = (t + 3) // 4 - 1 + (t == 0).astype(jnp.int32)
            r = (t + 3) % 4
            size = jnp.minimum(jnp.where(r < 2, 2 * g + 2, 2 * g + 1), span)
            d = jnp.where(t == 0, 0, jnp.where(r % 2 == 0, size, -size))
            valid = jnp.logical_and(mine + d >= 0, mine + d < total)

            @pl.when(jnp.logical_and(valid, d != 0))
            def _():
                send_to(buf, send, recv, span + d, span + d, 0, chip, other).wait_recv()

                @pl.when(size % 2 == 0)
                def _():
                    relay(buf, send, recv, d).start()

            @pl.when(valid)
            def _():
                use(d)
            return 0

        lax.fori_loop(0, 2 * span + 1, turn, 0)

    def finish(buf, send, recv):
        own_sends(buf, send, recv, lambda copy: copy.wait_send())
        for apart in range(1, reach + 1):
            for d in (2 * apart, -2 * apart):
                @pl.when(jnp.logical_and(mine + d >= 0, mine + d < total))
                def _(d=d):
                    relay(buf, send, recv, d).wait_send()

    near_f = pts[span, 0:blk, :].astype(jnp.float32).T
    near_t[...] = near_f.astype(jnp.bfloat16)
    near_sq = -c2 * jnp.sum(near_f * near_f, axis=0, keepdims=True)
    degree_ref[...] = jnp.zeros_like(degree_ref)
    step = 128

    def make_tile(d):
        flag_row = pts[span + jnp.minimum(d, 0), blk:blk + PAD, :].astype(jnp.float32)
        which = jnp.where(d == 0, feats - 1, jnp.abs(d) - 1)
        live = jnp.sum(jnp.where(lane == which, flag_row, 0.0)[0:1], axis=1, keepdims=True)
        near_term = near_sq + (1.0 - live) * -1.0e4

        def part(i, sums):
            at = pl.ds(pl.multiple_of(i * step, step), step)
            far = pts[span + d, at, :]
            far_f = far.astype(jnp.float32)
            far_sq = -c2 * jnp.sum(far_f * far_f, axis=1, keepdims=True)
            inner = jnp.dot(far, near_t[...], preferred_element_type=jnp.float32)
            tile = jnp.exp2((2.0 * c2) * inner + far_sq + near_term).astype(jnp.bfloat16)
            tiles[span + d, at, :] = tile
            return sums + jnp.sum(tile.astype(jnp.float32), axis=0, keepdims=True)

        degree_ref[...] += lax.fori_loop(0, blk // step, part, jnp.zeros((1, blk), jnp.float32))

    exchange(pts, pts_send, pts_recv, make_tile)
    inverse_root = lax.rsqrt(degree_ref[...])
    current = start_ref[...].T

    for it in range(STEPS):
        ebuf, esend, erecv = emb.at[it], emb_send.at[it], emb_recv.at[it]
        ebuf[span] = (inverse_root * current).astype(jnp.bfloat16)
        acc[...] = jnp.zeros_like(acc)

        def product(d):
            acc[...] += jnp.dot(ebuf[span + d], tiles[span + d], preferred_element_type=jnp.float32)

        exchange(ebuf, esend, erecv, product)
        y_t[...] = inverse_root * acc[...]
        local = lax.dot_general(y_t[...], y_t[...], (((1,), (1,)), ((), ())),
                                precision=lax.Precision.HIGHEST, preferred_element_type=jnp.float32)
        half = width // 2
        quarter = half // 2
        gram[it] = jnp.concatenate([local[0:half], local[half:width]], axis=1)
        own = pl.ds(pl.multiple_of(core * quarter, quarter), quarter)
        its = pl.ds(pl.multiple_of(other * quarter, quarter), quarter)
        first = pltpu.make_async_remote_copy(
            src_ref=gram.at[it, its], dst_ref=gram_near.at[it],
            send_sem=gsend.at[it, 0], recv_sem=grecv.at[it, 0],
            device_id=(group, chip, other), device_id_type=MESH)
        first.start()
        first.wait_recv()
        gram_all[it, chip] = gram[it, own] + gram_near[it]

        def scatter(o):
            to = lax.rem(chip + o, rows_n)
            return pltpu.make_async_remote_copy(
                src_ref=gram_all.at[it, chip], dst_ref=gram_all.at[it, chip],
                send_sem=gall_send.at[it, o], recv_sem=gall_recv.at[it, chip],
                device_id=(group, to, core), device_id_type=MESH)

        def start_one(o, _):
            scatter(o).start()
            return 0

        lax.fori_loop(1, rows_n, start_one, 0)

        def await_one(o, _):
            source = lax.rem(chip + o, rows_n)
            pltpu.make_async_remote_copy(
                src_ref=gram_all.at[it, source], dst_ref=gram_all.at[it, source],
                send_sem=gall_send.at[it, o], recv_sem=gall_recv.at[it, source],
                device_id=(group, source, core), device_id_type=MESH).wait_recv()
            return 0

        lax.fori_loop(1, rows_n, await_one, 0)
        gram_sum[it, own] = jnp.sum(gram_all[it], axis=0)
        last = pltpu.make_async_remote_copy(
            src_ref=gram_sum.at[it, own], dst_ref=gram_sum.at[it, own],
            send_sem=gsend.at[it, 1], recv_sem=grecv.at[it, 1],
            device_id=(group, chip, other), device_id_type=MESH)
        last.start()
        last.wait_recv()
        packed = gram_sum[it] * (1.0 / (blk * total))
        whole = jnp.concatenate([packed[:, 0:width], packed[:, width:2 * width]], axis=0)
        current = jnp.dot(inverse_cholesky(whole), y_t[...],
                          precision=lax.Precision.HIGHEST, preferred_element_type=jnp.float32)
        first.wait_send()
        last.wait_send()

        def sent_one(o, _):
            scatter(o).wait_send()
            return 0

        lax.fori_loop(1, rows_n, sent_one, 0)

    out_ref[...] = current.T
    finish(pts, pts_send, pts_recv)
    for it in range(STEPS):
        finish(emb.at[it], emb_send.at[it], emb_recv.at[it])


def per_device(rows_n, points, start, pair_mask):
    blk, feats = points.shape
    width = start.shape[1]
    span = pair_mask.shape[1]
    slots = 2 * span + 1
    vmem = pl.BlockSpec(memory_space=pltpu.VMEM)
    embedding, degree = pl.pallas_call(
        functools.partial(kernel, rows_n, span),
        out_shape=(jax.ShapeDtypeStruct((blk, width), jnp.float32), jax.ShapeDtypeStruct((1, blk), jnp.float32)),
        in_specs=[vmem, vmem, pl.BlockSpec(memory_space=pltpu.SMEM)],
        out_specs=(vmem, vmem),
        scratch_shapes=[
            pltpu.VMEM((slots, blk + PAD, feats), jnp.bfloat16),
            pltpu.VMEM((feats, blk), jnp.bfloat16),
            pltpu.VMEM((slots, blk, blk), jnp.bfloat16),
            pltpu.VMEM((STEPS, slots, width, blk), jnp.bfloat16),
            pltpu.VMEM((width, blk), jnp.float32),
            pltpu.VMEM((width, blk), jnp.float32),
            pltpu.VMEM((STEPS, width // 2, 2 * width), jnp.float32),
            pltpu.VMEM((STEPS, width // 4, 2 * width), jnp.float32),
            pltpu.VMEM((STEPS, rows_n, width // 4, 2 * width), jnp.float32),
            pltpu.VMEM((STEPS, width // 2, 2 * width), jnp.float32),
            pltpu.SemaphoreType.DMA((slots + 1,)),
            pltpu.SemaphoreType.DMA((slots,)),
            pltpu.SemaphoreType.DMA((STEPS, slots + 1)),
            pltpu.SemaphoreType.DMA((STEPS, slots)),
            pltpu.SemaphoreType.DMA((STEPS, 2)),
            pltpu.SemaphoreType.DMA((STEPS, 2)),
            pltpu.SemaphoreType.DMA((STEPS, rows_n)),
            pltpu.SemaphoreType.DMA((STEPS, rows_n)),
        ],
        compiler_params=pltpu.CompilerParams(
            collective_id=0, has_side_effects=True, vmem_limit_bytes=56 * 1024 * 1024),
    )(points, start, pair_mask)
    return embedding, degree[0]


def solution(mesh):
    rows = P(("groups", "row", "col"), None)
    return jax.shard_map(
        functools.partial(per_device, mesh.shape["row"]), mesh=mesh, in_specs=(rows, rows, rows),
        out_specs=(rows, P(("groups", "row", "col"))), check_vma=False)
```

```python
import functools
import math

import jax
import jax.numpy as jnp
from jax import lax
from jax.experimental import pallas as pl
from jax.experimental.pallas import tpu as pltpu
from jax.sharding import PartitionSpec as P

STEPS = 2
MESH = pl.DeviceIdType.MESH
PAD = 16
RANGE = 8.0


def inverse_cholesky(gram):
    n = gram.shape[0]
    rows = lax.broadcasted_iota(jnp.int32, (n, 2 * n), 0)
    lanes = lax.broadcasted_iota(jnp.int32, (n, 2 * n), 1)
    eye = jnp.where(lanes == rows + n, 1.0, 0.0)
    mat = jnp.concatenate([gram, jnp.zeros_like(gram)], axis=1) + eye
    diag = jnp.ones((n, 1), jnp.float32)
    row_of = lax.broadcasted_iota(jnp.int32, (n, 1), 0)
    for k in range(n):
        pivot = mat[k:k + 1, k:k + 1]
        diag = jnp.where(row_of == k, pivot, diag)
        if k < n - 1:
            line = mat[k:k + 1, :] * (1.0 / pivot)
            column = jnp.where(row_of > k, mat[:, k:k + 1], 0.0)
            mat = mat - column * line
    return mat[:, n:] * lax.rsqrt(diag)


def kernel(rows_n, span, points_ref, start_ref, mask_ref, out_ref, degree_ref,
           pts, near_t, tiles, emb, acc, y_t, gram, gram_near, gram_all, gram_sum,
           pts_send, pts_recv, emb_send, emb_recv, gsend, grecv, gall_send, gall_recv):
    group = lax.axis_index("groups")
    chip = lax.axis_index("row")
    core = lax.axis_index("col")
    mine = 2 * chip + core
    total = 2 * rows_n
    other = 1 - core
    side = 1 - 2 * core
    blk = points_ref.shape[0]
    width = start_ref.shape[1]
    feats = points_ref.shape[1]
    reach = span // 2
    c2 = 4.0 / feats * math.log2(math.e)

    far_chip = chip + (reach + 1) * (2 * core - 1)
    has_far = jnp.logical_and(far_chip >= 0, far_chip < rows_n)

    barrier = pltpu.get_barrier_semaphore()

    def greet(o, _):
        pl.semaphore_signal(barrier, inc=1, device_id=(group, lax.rem(chip + o, rows_n), core), device_id_type=MESH)
        return 0

    lax.fori_loop(1, rows_n, greet, 0)
    pl.semaphore_signal(barrier, inc=1, device_id=(group, chip, other), device_id_type=MESH)

    @pl.when(has_far)
    def _():
        pl.semaphore_signal(barrier, inc=1, device_id=(group, far_chip, other), device_id_type=MESH)

    pts[span, 0:blk, :] = jnp.round(points_ref[...] * (32767.0 / RANGE)).astype(jnp.int32).astype(jnp.int16)
    lane = lax.broadcasted_iota(jnp.int32, (PAD, feats), 1)
    flags = jnp.where(lane == feats - 1, 1, 0)
    for i in range(span):
        flags = jnp.where(lane == i, mask_ref[0, i], flags)
    pts[span, blk:blk + PAD, :] = flags.astype(jnp.int16)

    pl.semaphore_wait(barrier, rows_n + has_far.astype(jnp.int32))

    def send_to(buf, send, recv, from_slot, to_slot, sem, to_chip, to_core):
        return pltpu.make_async_remote_copy(
            src_ref=buf.at[from_slot], dst_ref=buf.at[to_slot],
            send_sem=send.at[sem], recv_sem=recv.at[to_slot],
            device_id=(group, to_chip, to_core), device_id_type=MESH)

    def own_sends(buf, send, recv, action):
        def near(apart):
            @pl.when(jnp.logical_and(chip + apart >= 0, chip + apart < rows_n))
            def _():
                action(send_to(buf, send, recv, span, span - 2 * apart, span + 2 * apart, chip + apart, core))

        action(send_to(buf, send, recv, span, span - side, span, chip, other))
        for apart in range(1, reach + 1):
            near(apart)
            near(-apart)

        @pl.when(has_far)
        def _():
            action(send_to(buf, send, recv, span, span - span * (2 * core - 1), 2 * span + 1, far_chip, other))

    def relay(buf, send, recv, d):
        return send_to(buf, send, recv, span + d, span + d - side, span + d + 1, chip, other)

    def exchange(buf, send, recv, use):
        own_sends(buf, send, recv, lambda copy: copy.start())

        def turn(t, _):
            g = (t + 3) // 4 - 1 + (t == 0).astype(jnp.int32)
            r = (t + 3) % 4
            size = jnp.minimum(jnp.where(r < 2, 2 * g + 2, 2 * g + 1), span)
            d = jnp.where(t == 0, 0, jnp.where(r % 2 == 0, size, -size))
            valid = jnp.logical_and(mine + d >= 0, mine + d < total)

            @pl.when(jnp.logical_and(valid, d != 0))
            def _():
                send_to(buf, send, recv, span + d, span + d, 0, chip, other).wait_recv()

                @pl.when(size % 2 == 0)
                def _():
                    relay(buf, send, recv, d).start()

            @pl.when(valid)
            def _():
                use(d)
            return 0

        lax.fori_loop(0, 2 * span + 1, turn, 0)

    def finish(buf, send, recv):
        own_sends(buf, send, recv, lambda copy: copy.wait_send())
        for apart in range(1, reach + 1):
            for d in (2 * apart, -2 * apart):
                @pl.when(jnp.logical_and(mine + d >= 0, mine + d < total))
                def _(d=d):
                    relay(buf, send, recv, d).wait_send()

    def decode(coded):
        return coded.astype(jnp.int32).astype(jnp.float32) * (RANGE / 32767.0)

    def split(exact):
        high = exact.astype(jnp.bfloat16)
        return high, (exact - high.astype(jnp.float32)).astype(jnp.bfloat16)

    near_f = decode(pts[span, 0:blk, :]).T
    near_high, near_low = split(near_f)
    near_t[0:feats] = near_high
    near_t[feats:2 * feats] = near_high
    near_t[2 * feats:3 * feats] = near_low
    near_t[3 * feats:4 * feats] = near_low
    near_sq = -c2 * jnp.sum(near_f * near_f, axis=0, keepdims=True)
    degree_ref[...] = jnp.zeros_like(degree_ref)
    step = 128

    def make_tile(d):
        flag_row = pts[span + jnp.minimum(d, 0), blk:blk + PAD, :].astype(jnp.int32).astype(jnp.float32)
        which = jnp.where(d == 0, feats - 1, jnp.abs(d) - 1)
        live = jnp.sum(jnp.where(lane == which, flag_row, 0.0)[0:1], axis=1, keepdims=True)
        near_term = near_sq + (1.0 - live) * -1.0e4

        def part(i, sums):
            at = pl.ds(pl.multiple_of(i * step, step), step)
            far_f = decode(pts[span + d, at, :])
            far_high, far_low = split(far_f)
            far = jnp.concatenate([far_high, far_low, far_high, far_low], axis=1)
            far_sq = -c2 * jnp.sum(far_f * far_f, axis=1, keepdims=True)
            inner = jnp.dot(far, near_t[...], preferred_element_type=jnp.float32)
            tile = jnp.exp2((2.0 * c2) * inner + far_sq + near_term).astype(jnp.bfloat16)
            tiles[span + d, at, :] = tile
            return sums + jnp.sum(tile.astype(jnp.float32), axis=0, keepdims=True)

        degree_ref[...] += lax.fori_loop(0, blk // step, part, jnp.zeros((1, blk), jnp.float32))

    exchange(pts, pts_send, pts_recv, make_tile)
    inverse_root = lax.rsqrt(degree_ref[...])
    current = start_ref[...].T

    for it in range(STEPS):
        ebuf, esend, erecv = emb.at[it], emb_send.at[it], emb_recv.at[it]
        ebuf[span] = (inverse_root * current).astype(jnp.bfloat16)
        acc[...] = jnp.zeros_like(acc)

        def product(d):
            acc[...] += jnp.dot(ebuf[span + d], tiles[span + d], preferred_element_type=jnp.float32)

        exchange(ebuf, esend, erecv, product)
        y_t[...] = inverse_root * acc[...]
        local = lax.dot_general(y_t[...], y_t[...], (((1,), (1,)), ((), ())),
                                precision=lax.Precision.HIGHEST, preferred_element_type=jnp.float32)
        half = width // 2
        quarter = half // 2
        gram[it] = jnp.concatenate([local[0:half], local[half:width]], axis=1)
        own = pl.ds(pl.multiple_of(core * quarter, quarter), quarter)
        its = pl.ds(pl.multiple_of(other * quarter, quarter), quarter)
        first = pltpu.make_async_remote_copy(
            src_ref=gram.at[it, its], dst_ref=gram_near.at[it],
            send_sem=gsend.at[it, 0], recv_sem=grecv.at[it, 0],
            device_id=(group, chip, other), device_id_type=MESH)
        first.start()
        first.wait_recv()
        gram_all[it, chip] = gram[it, own] + gram_near[it]

        def scatter(o):
            to = lax.rem(chip + o, rows_n)
            return pltpu.make_async_remote_copy(
                src_ref=gram_all.at[it, chip], dst_ref=gram_all.at[it, chip],
                send_sem=gall_send.at[it, o], recv_sem=gall_recv.at[it, chip],
                device_id=(group, to, core), device_id_type=MESH)

        def start_one(o, _):
            scatter(o).start()
            return 0

        lax.fori_loop(1, rows_n, start_one, 0)

        def await_one(o, _):
            source = lax.rem(chip + o, rows_n)
            pltpu.make_async_remote_copy(
                src_ref=gram_all.at[it, source], dst_ref=gram_all.at[it, source],
                send_sem=gall_send.at[it, o], recv_sem=gall_recv.at[it, source],
                device_id=(group, source, core), device_id_type=MESH).wait_recv()
            return 0

        lax.fori_loop(1, rows_n, await_one, 0)
        gram_sum[it, own] = jnp.sum(gram_all[it], axis=0)
        last = pltpu.make_async_remote_copy(
            src_ref=gram_sum.at[it, own], dst_ref=gram_sum.at[it, own],
            send_sem=gsend.at[it, 1], recv_sem=grecv.at[it, 1],
            device_id=(group, chip, other), device_id_type=MESH)
        last.start()
        last.wait_recv()
        packed = gram_sum[it] * (1.0 / (blk * total))
        whole = jnp.concatenate([packed[:, 0:width], packed[:, width:2 * width]], axis=0)
        current = jnp.dot(inverse_cholesky(whole), y_t[...],
                          precision=lax.Precision.HIGHEST, preferred_element_type=jnp.float32)
        first.wait_send()
        last.wait_send()

        def sent_one(o, _):
            scatter(o).wait_send()
            return 0

        lax.fori_loop(1, rows_n, sent_one, 0)

    out_ref[...] = current.T
    finish(pts, pts_send, pts_recv)
    for it in range(STEPS):
        finish(emb.at[it], emb_send.at[it], emb_recv.at[it])


def per_device(rows_n, points, start, pair_mask):
    blk, feats = points.shape
    width = start.shape[1]
    span = pair_mask.shape[1]
    slots = 2 * span + 1
    vmem = pl.BlockSpec(memory_space=pltpu.VMEM)
    embedding, degree = pl.pallas_call(
        functools.partial(kernel, rows_n, span),
        out_shape=(jax.ShapeDtypeStruct((blk, width), jnp.float32), jax.ShapeDtypeStruct((1, blk), jnp.float32)),
        in_specs=[vmem, vmem, pl.BlockSpec(memory_space=pltpu.SMEM)],
        out_specs=(vmem, vmem),
        scratch_shapes=[
            pltpu.VMEM((slots, blk + PAD, feats), jnp.int16),
            pltpu.VMEM((4 * feats, blk), jnp.bfloat16),
            pltpu.VMEM((slots, blk, blk), jnp.bfloat16),
            pltpu.VMEM((STEPS, slots, width, blk), jnp.bfloat16),
            pltpu.VMEM((width, blk), jnp.float32),
            pltpu.VMEM((width, blk), jnp.float32),
            pltpu.VMEM((STEPS, width // 2, 2 * width), jnp.float32),
            pltpu.VMEM((STEPS, width // 4, 2 * width), jnp.float32),
            pltpu.VMEM((STEPS, rows_n, width // 4, 2 * width), jnp.float32),
            pltpu.VMEM((STEPS, width // 2, 2 * width), jnp.float32),
            pltpu.SemaphoreType.DMA((slots + 1,)),
            pltpu.SemaphoreType.DMA((slots,)),
            pltpu.SemaphoreType.DMA((STEPS, slots + 1)),
            pltpu.SemaphoreType.DMA((STEPS, slots)),
            pltpu.SemaphoreType.DMA((STEPS, 2)),
            pltpu.SemaphoreType.DMA((STEPS, 2)),
            pltpu.SemaphoreType.DMA((STEPS, rows_n)),
            pltpu.SemaphoreType.DMA((STEPS, rows_n)),
        ],
        compiler_params=pltpu.CompilerParams(
            collective_id=0, has_side_effects=True, vmem_limit_bytes=56 * 1024 * 1024),
    )(points, start, pair_mask)
    return embedding, degree[0]


def solution(mesh):
    rows = P(("groups", "row", "col"), None)
    return jax.shard_map(
        functools.partial(per_device, mesh.shape["row"]), mesh=mesh, in_specs=(rows, rows, rows),
        out_specs=(rows, P(("groups", "row", "col"))), check_vma=False)
```

```python
import functools
import math

import jax
import jax.numpy as jnp
from jax import lax
from jax.experimental import pallas as pl
from jax.experimental.pallas import tpu as pltpu
from jax.sharding import PartitionSpec as P

STEPS = 2
MESH = pl.DeviceIdType.MESH
PAD = 16
RANGE = 8.0


def inverse_cholesky(gram):
    n = gram.shape[0]
    group = 4
    rows = lax.broadcasted_iota(jnp.int32, (n, 2 * n), 0)
    lanes = lax.broadcasted_iota(jnp.int32, (n, 2 * n), 1)
    mat = jnp.concatenate([gram, jnp.zeros_like(gram)], axis=1) + jnp.where(lanes == rows + n, 1.0, 0.0)
    done = []
    for k in range(0, n, group):
        lines = [mat[k + i:k + i + 1, :] for i in range(group)]
        columns = [jnp.broadcast_to(mat[:, k + i:k + i + 1], (n, 2 * n)) for i in range(group)]
        corner = [[columns[j][k + i:k + i + 1, :] for j in range(group)] for i in range(group)]
        for i in range(group):
            inverse = 1.0 / corner[i][i]
            for j in range(i + 1, group):
                ratio = corner[i][j] * inverse
                for m in range(j, group):
                    corner[j][m] = corner[j][m] - ratio * corner[i][m]
                lines[j] = lines[j] - ratio * lines[i]
                columns[j] = columns[j] - ratio * columns[i]
            done.append(lines[i] * lax.rsqrt(corner[i][i]))
            if k + group < n:
                mat = mat - columns[i] * (lines[i] * inverse)
    return jnp.concatenate(done, axis=0)[:, n:]


def kernel(rows_n, span, points_ref, start_ref, mask_ref, out_ref, degree_ref,
           pts, near_t, far, tiles, emb, acc, y_t, gram, gram_near, gram_all, gram_sum,
           pts_send, pts_recv, emb_send, emb_recv, gsend, grecv, gall_send, gall_recv):
    group = lax.axis_index("groups")
    chip = lax.axis_index("row")
    core = lax.axis_index("col")
    mine = 2 * chip + core
    total = 2 * rows_n
    other = 1 - core
    side = 1 - 2 * core
    blk = points_ref.shape[0]
    width = start_ref.shape[1]
    feats = points_ref.shape[1]
    reach = span // 2
    c2 = 4.0 / feats * math.log2(math.e)

    far_chip = chip + (reach + 1) * (2 * core - 1)
    has_far = jnp.logical_and(far_chip >= 0, far_chip < rows_n)

    barrier = pltpu.get_barrier_semaphore()

    def greet(o, _):
        pl.semaphore_signal(barrier, inc=1, device_id=(group, lax.rem(chip + o, rows_n), core), device_id_type=MESH)
        return 0

    lax.fori_loop(1, rows_n, greet, 0)
    pl.semaphore_signal(barrier, inc=1, device_id=(group, chip, other), device_id_type=MESH)

    @pl.when(has_far)
    def _():
        pl.semaphore_signal(barrier, inc=1, device_id=(group, far_chip, other), device_id_type=MESH)

    pts[span, 0:blk, :] = jnp.round(points_ref[...] * (32767.0 / RANGE)).astype(jnp.int32).astype(jnp.int16)
    lane = lax.broadcasted_iota(jnp.int32, (PAD, feats), 1)
    flags = jnp.where(lane == feats - 1, 1, 0)
    for i in range(span):
        flags = jnp.where(lane == i, mask_ref[0, i], flags)
    pts[span, blk:blk + PAD, :] = flags.astype(jnp.int16)

    pl.semaphore_wait(barrier, rows_n + has_far.astype(jnp.int32))

    def send_to(buf, send, recv, from_slot, to_slot, sem, to_chip, to_core):
        return pltpu.make_async_remote_copy(
            src_ref=buf.at[from_slot], dst_ref=buf.at[to_slot],
            send_sem=send.at[sem], recv_sem=recv.at[to_slot],
            device_id=(group, to_chip, to_core), device_id_type=MESH)

    def own_sends(buf, send, recv, action):
        def near(apart):
            @pl.when(jnp.logical_and(chip + apart >= 0, chip + apart < rows_n))
            def _():
                action(send_to(buf, send, recv, span, span - 2 * apart, span + 2 * apart, chip + apart, core))

        action(send_to(buf, send, recv, span, span - side, span, chip, other))
        for apart in range(1, reach + 1):
            near(apart)
            near(-apart)

        @pl.when(has_far)
        def _():
            action(send_to(buf, send, recv, span, span - span * (2 * core - 1), 2 * span + 1, far_chip, other))

    def relay(buf, send, recv, d):
        return send_to(buf, send, recv, span + d, span + d - side, span + d + 1, chip, other)

    def exchange(buf, send, recv, use):
        own_sends(buf, send, recv, lambda copy: copy.start())

        def turn(t, _):
            g = (t + 3) // 4 - 1 + (t == 0).astype(jnp.int32)
            r = (t + 3) % 4
            size = jnp.minimum(jnp.where(r < 2, 2 * g + 2, 2 * g + 1), span)
            d = jnp.where(t == 0, 0, jnp.where(r % 2 == 0, size, -size))
            valid = jnp.logical_and(mine + d >= 0, mine + d < total)

            @pl.when(jnp.logical_and(valid, d != 0))
            def _():
                send_to(buf, send, recv, span + d, span + d, 0, chip, other).wait_recv()

                @pl.when(size % 2 == 0)
                def _():
                    relay(buf, send, recv, d).start()

            @pl.when(valid)
            def _():
                use(d)
            return 0

        lax.fori_loop(0, 2 * span + 1, turn, 0)

    def finish(buf, send, recv):
        own_sends(buf, send, recv, lambda copy: copy.wait_send())
        for apart in range(1, reach + 1):
            for d in (2 * apart, -2 * apart):
                @pl.when(jnp.logical_and(mine + d >= 0, mine + d < total))
                def _(d=d):
                    relay(buf, send, recv, d).wait_send()

    def decode(coded):
        return coded.astype(jnp.int32).astype(jnp.float32) * (RANGE / 32767.0)

    def split(exact):
        high = exact.astype(jnp.bfloat16)
        return high, (exact - high.astype(jnp.float32)).astype(jnp.bfloat16)

    near_f = decode(pts[span, 0:blk, :]).T
    near_high, near_low = split((2.0 * c2) * near_f)
    near_t[0:feats] = near_high
    near_t[feats:2 * feats] = near_high
    near_t[2 * feats:3 * feats] = near_low
    near_t[3 * feats:4 * feats] = near_low
    near_sq = -c2 * jnp.sum(near_f * near_f, axis=0, keepdims=True)
    degree_ref[...] = jnp.zeros_like(degree_ref)
    step = min(256, blk)

    def make_tile(d):
        flag_row = pts[span + jnp.minimum(d, 0), blk:blk + PAD, :].astype(jnp.int32).astype(jnp.float32)
        which = jnp.where(d == 0, feats - 1, jnp.abs(d) - 1)
        live = jnp.sum(jnp.where(lane == which, flag_row, 0.0)[0:1], axis=1, keepdims=True)
        near_term = near_sq + (1.0 - live) * -1.0e4

        far_f = decode(pts[span + d, 0:blk, :])
        far_sq = -c2 * jnp.sum(far_f * far_f, axis=1, keepdims=True)
        far_high, far_low = split(far_f)
        far[:, 0:feats] = far_high
        far[:, feats:2 * feats] = far_low
        for at in range(0, blk, step):
            here = slice(at, at + step)
            inner = (jnp.dot(far[...], near_t[0:2 * feats, here], preferred_element_type=jnp.float32)
                     + jnp.dot(far[...], near_t[2 * feats:4 * feats, here], preferred_element_type=jnp.float32))
            tile = jnp.exp2(inner + far_sq + near_term[:, here]).astype(jnp.bfloat16)
            tiles[span + d, :, here] = tile
            degree_ref[:, here] += jnp.sum(tile.astype(jnp.float32), axis=0, keepdims=True)

    exchange(pts, pts_send, pts_recv, make_tile)
    inverse_root = lax.rsqrt(degree_ref[...])
    current = start_ref[...].T

    for it in range(STEPS):
        ebuf, esend, erecv = emb.at[it], emb_send.at[it], emb_recv.at[it]
        ebuf[span] = (inverse_root * current).astype(jnp.bfloat16)
        acc[...] = jnp.zeros_like(acc)

        def product(d):
            acc[...] += jnp.dot(ebuf[span + d], tiles[span + d], preferred_element_type=jnp.float32)

        exchange(ebuf, esend, erecv, product)
        y_t[...] = inverse_root * acc[...]
        local = lax.dot_general(y_t[...], y_t[...], (((1,), (1,)), ((), ())),
                                precision=lax.Precision.HIGHEST, preferred_element_type=jnp.float32)
        half = width // 2
        quarter = half // 2
        gram[it] = jnp.concatenate([local[0:half], local[half:width]], axis=1)
        own = pl.ds(pl.multiple_of(core * quarter, quarter), quarter)
        its = pl.ds(pl.multiple_of(other * quarter, quarter), quarter)
        first = pltpu.make_async_remote_copy(
            src_ref=gram.at[it, its], dst_ref=gram_near.at[it],
            send_sem=gsend.at[it, 0], recv_sem=grecv.at[it, 0],
            device_id=(group, chip, other), device_id_type=MESH)
        first.start()
        first.wait_recv()
        gram_all[it, chip] = gram[it, own] + gram_near[it]

        def scatter(o):
            to = lax.rem(chip + o, rows_n)
            return pltpu.make_async_remote_copy(
                src_ref=gram_all.at[it, chip], dst_ref=gram_all.at[it, chip],
                send_sem=gall_send.at[it, o], recv_sem=gall_recv.at[it, chip],
                device_id=(group, to, core), device_id_type=MESH)

        def start_one(o, _):
            scatter(o).start()
            return 0

        lax.fori_loop(1, rows_n, start_one, 0)

        def await_one(o, _):
            source = lax.rem(chip + o, rows_n)
            pltpu.make_async_remote_copy(
                src_ref=gram_all.at[it, source], dst_ref=gram_all.at[it, source],
                send_sem=gall_send.at[it, o], recv_sem=gall_recv.at[it, source],
                device_id=(group, source, core), device_id_type=MESH).wait_recv()
            return 0

        lax.fori_loop(1, rows_n, await_one, 0)
        gram_sum[it, own] = jnp.sum(gram_all[it], axis=0)
        last = pltpu.make_async_remote_copy(
            src_ref=gram_sum.at[it, own], dst_ref=gram_sum.at[it, own],
            send_sem=gsend.at[it, 1], recv_sem=grecv.at[it, 1],
            device_id=(group, chip, other), device_id_type=MESH)
        last.start()
        last.wait_recv()
        packed = gram_sum[it] * (1.0 / (blk * total))
        whole = jnp.concatenate([packed[:, 0:width], packed[:, width:2 * width]], axis=0)
        current = jnp.dot(inverse_cholesky(whole), y_t[...],
                          precision=lax.Precision.HIGHEST, preferred_element_type=jnp.float32)
        first.wait_send()
        last.wait_send()

        def sent_one(o, _):
            scatter(o).wait_send()
            return 0

        lax.fori_loop(1, rows_n, sent_one, 0)

    out_ref[...] = current.T
    finish(pts, pts_send, pts_recv)
    for it in range(STEPS):
        finish(emb.at[it], emb_send.at[it], emb_recv.at[it])


def per_device(rows_n, points, start, pair_mask):
    blk, feats = points.shape
    width = start.shape[1]
    span = pair_mask.shape[1]
    slots = 2 * span + 1
    vmem = pl.BlockSpec(memory_space=pltpu.VMEM)
    embedding, degree = pl.pallas_call(
        functools.partial(kernel, rows_n, span),
        out_shape=(jax.ShapeDtypeStruct((blk, width), jnp.float32), jax.ShapeDtypeStruct((1, blk), jnp.float32)),
        in_specs=[vmem, vmem, pl.BlockSpec(memory_space=pltpu.SMEM)],
        out_specs=(vmem, vmem),
        scratch_shapes=[
            pltpu.VMEM((slots, blk + PAD, feats), jnp.int16),
            pltpu.VMEM((4 * feats, blk), jnp.bfloat16),
            pltpu.VMEM((blk, 2 * feats), jnp.bfloat16),
            pltpu.VMEM((slots, blk, blk), jnp.bfloat16),
            pltpu.VMEM((STEPS, slots, width, blk), jnp.bfloat16),
            pltpu.VMEM((width, blk), jnp.float32),
            pltpu.VMEM((width, blk), jnp.float32),
            pltpu.VMEM((STEPS, width // 2, 2 * width), jnp.float32),
            pltpu.VMEM((STEPS, width // 4, 2 * width), jnp.float32),
            pltpu.VMEM((STEPS, rows_n, width // 4, 2 * width), jnp.float32),
            pltpu.VMEM((STEPS, width // 2, 2 * width), jnp.float32),
            pltpu.SemaphoreType.DMA((slots + 1,)),
            pltpu.SemaphoreType.DMA((slots,)),
            pltpu.SemaphoreType.DMA((STEPS, slots + 1)),
            pltpu.SemaphoreType.DMA((STEPS, slots)),
            pltpu.SemaphoreType.DMA((STEPS, 2)),
            pltpu.SemaphoreType.DMA((STEPS, 2)),
            pltpu.SemaphoreType.DMA((STEPS, rows_n)),
            pltpu.SemaphoreType.DMA((STEPS, rows_n)),
        ],
        compiler_params=pltpu.CompilerParams(
            collective_id=0, has_side_effects=True, vmem_limit_bytes=56 * 1024 * 1024),
    )(points, start, pair_mask)
    return embedding, degree[0]


def solution(mesh):
    rows = P(("groups", "row", "col"), None)
    return jax.shard_map(
        functools.partial(per_device, mesh.shape["row"]), mesh=mesh, in_specs=(rows, rows, rows),
        out_specs=(rows, P(("groups", "row", "col"))), check_vma=False)
```

```python
import functools
import math

import jax
import jax.numpy as jnp
from jax import lax
from jax.experimental import pallas as pl
from jax.experimental.pallas import tpu as pltpu
from jax.sharding import PartitionSpec as P

STEPS = 2
MESH = pl.DeviceIdType.MESH
PAD = 16
RANGE = 8.0


def inverse_cholesky(gram):
    n = gram.shape[0]
    group = 4
    rows = lax.broadcasted_iota(jnp.int32, (n, 2 * n), 0)
    lanes = lax.broadcasted_iota(jnp.int32, (n, 2 * n), 1)
    mat = jnp.concatenate([gram, jnp.zeros_like(gram)], axis=1) + jnp.where(lanes == rows + n, 1.0, 0.0)
    done = []
    for k in range(0, n, group):
        lines = [mat[k + i:k + i + 1, :] for i in range(group)]
        columns = [jnp.broadcast_to(mat[:, k + i:k + i + 1], (n, 2 * n)) for i in range(group)]
        corner = [[columns[j][k + i:k + i + 1, :] for j in range(group)] for i in range(group)]
        for i in range(group):
            inverse = 1.0 / corner[i][i]
            for j in range(i + 1, group):
                ratio = corner[i][j] * inverse
                for m in range(j, group):
                    corner[j][m] = corner[j][m] - ratio * corner[i][m]
                lines[j] = lines[j] - ratio * lines[i]
                columns[j] = columns[j] - ratio * columns[i]
            done.append(lines[i] * lax.rsqrt(corner[i][i]))
            if k + group < n:
                mat = mat - columns[i] * (lines[i] * inverse)
    return jnp.concatenate(done, axis=0)[:, n:]


def kernel(rows_n, span, points_ref, start_ref, mask_ref, out_ref, degree_ref,
           pts, near_t, far, tiles, emb, acc, y_t, gram, gram_near, gram_all, gram_sum,
           pts_send, pts_recv, emb_send, emb_recv, gsend, grecv, gall_send, gall_recv):
    group = lax.axis_index("groups")
    chip = lax.axis_index("row")
    core = lax.axis_index("col")
    mine = 2 * chip + core
    total = 2 * rows_n
    other = 1 - core
    side = 1 - 2 * core
    blk = points_ref.shape[0]
    width = start_ref.shape[1]
    feats = points_ref.shape[1]
    reach = span // 2
    c2 = 4.0 / feats * math.log2(math.e)

    far_chip = chip + (reach + 1) * (2 * core - 1)
    has_far = jnp.logical_and(far_chip >= 0, far_chip < rows_n)

    barrier = pltpu.get_barrier_semaphore()

    def greet(o, _):
        pl.semaphore_signal(barrier, inc=1, device_id=(group, lax.rem(chip + o, rows_n), core), device_id_type=MESH)
        return 0

    lax.fori_loop(1, rows_n, greet, 0)
    pl.semaphore_signal(barrier, inc=1, device_id=(group, chip, other), device_id_type=MESH)

    @pl.when(has_far)
    def _():
        pl.semaphore_signal(barrier, inc=1, device_id=(group, far_chip, other), device_id_type=MESH)

    pts[span, 0:blk, :] = jnp.round(points_ref[...] * (32767.0 / RANGE)).astype(jnp.int32).astype(jnp.int16)
    lane = lax.broadcasted_iota(jnp.int32, (PAD, feats), 1)
    flags = jnp.where(lane == feats - 1, 1, 0)
    for i in range(span):
        flags = jnp.where(lane == i, mask_ref[0, i], flags)
    pts[span, blk:blk + PAD, :] = flags.astype(jnp.int16)

    pl.semaphore_wait(barrier, rows_n + has_far.astype(jnp.int32))

    def send_to(buf, send, recv, from_slot, to_slot, sem, to_chip, to_core):
        return pltpu.make_async_remote_copy(
            src_ref=buf.at[from_slot], dst_ref=buf.at[to_slot],
            send_sem=send.at[sem], recv_sem=recv.at[to_slot],
            device_id=(group, to_chip, to_core), device_id_type=MESH)

    def own_sends(buf, send, recv, action):
        def near(apart):
            @pl.when(jnp.logical_and(chip + apart >= 0, chip + apart < rows_n))
            def _():
                action(send_to(buf, send, recv, span, span - 2 * apart, span + 2 * apart, chip + apart, core))

        action(send_to(buf, send, recv, span, span - side, span, chip, other))
        for apart in range(1, reach + 1):
            near(apart)
            near(-apart)

        @pl.when(has_far)
        def _():
            action(send_to(buf, send, recv, span, span - span * (2 * core - 1), 2 * span + 1, far_chip, other))

    def relay(buf, send, recv, d):
        return send_to(buf, send, recv, span + d, span + d - side, span + d + 1, chip, other)

    def exchange(buf, send, recv, use):
        own_sends(buf, send, recv, lambda copy: copy.start())

        def turn(t, _):
            g = (t + 3) // 4 - 1 + (t == 0).astype(jnp.int32)
            r = (t + 3) % 4
            size = jnp.minimum(jnp.where(r < 2, 2 * g + 2, 2 * g + 1), span)
            d = jnp.where(t == 0, 0, jnp.where(r % 2 == 0, size, -size))
            d = jnp.where(t == 1, side, jnp.where(t == 4, -side, d))
            d = jnp.where(t == 2, 2, jnp.where(t == 3, -2, d))
            size = jnp.abs(d)
            valid = jnp.logical_and(mine + d >= 0, mine + d < total)

            @pl.when(jnp.logical_and(valid, d != 0))
            def _():
                send_to(buf, send, recv, span + d, span + d, 0, chip, other).wait_recv()

                @pl.when(size % 2 == 0)
                def _():
                    relay(buf, send, recv, d).start()

            @pl.when(valid)
            def _():
                use(d)
            return 0

        lax.fori_loop(0, 2 * span + 1, turn, 0)

    def finish(buf, send, recv):
        own_sends(buf, send, recv, lambda copy: copy.wait_send())
        for apart in range(1, reach + 1):
            for d in (2 * apart, -2 * apart):
                @pl.when(jnp.logical_and(mine + d >= 0, mine + d < total))
                def _(d=d):
                    relay(buf, send, recv, d).wait_send()

    def decode(coded):
        return coded.astype(jnp.int32).astype(jnp.float32) * (RANGE / 32767.0)

    def split(exact):
        high = exact.astype(jnp.bfloat16)
        return high, (exact - high.astype(jnp.float32)).astype(jnp.bfloat16)

    near_f = decode(pts[span, 0:blk, :]).T
    near_high, near_low = split((2.0 * c2) * near_f)
    near_t[0:feats] = near_high
    near_t[feats:2 * feats] = near_high
    near_t[2 * feats:3 * feats] = near_low
    near_t[3 * feats:4 * feats] = near_low
    near_sq = -c2 * jnp.sum(near_f * near_f, axis=0, keepdims=True)
    degree_ref[...] = jnp.zeros_like(degree_ref)
    step = min(256, blk)

    def make_tile(d):
        flag_row = pts[span + jnp.minimum(d, 0), blk:blk + PAD, :].astype(jnp.int32).astype(jnp.float32)
        which = jnp.where(d == 0, feats - 1, jnp.abs(d) - 1)
        live = jnp.sum(jnp.where(lane == which, flag_row, 0.0)[0:1], axis=1, keepdims=True)
        near_term = near_sq + (1.0 - live) * -1.0e4

        far_f = decode(pts[span + d, 0:blk, :])
        far_sq = -c2 * jnp.sum(far_f * far_f, axis=1, keepdims=True)
        far_high, far_low = split(far_f)
        far[:, 0:feats] = far_high
        far[:, feats:2 * feats] = far_low
        for at in range(0, blk, step):
            here = slice(at, at + step)
            inner = (jnp.dot(far[...], near_t[0:2 * feats, here], preferred_element_type=jnp.float32)
                     + jnp.dot(far[...], near_t[2 * feats:4 * feats, here], preferred_element_type=jnp.float32))
            tile = jnp.exp2(inner + far_sq + near_term[:, here]).astype(jnp.bfloat16)
            tiles[span + d, :, here] = tile
            degree_ref[:, here] += jnp.sum(tile.astype(jnp.float32), axis=0, keepdims=True)

    exchange(pts, pts_send, pts_recv, make_tile)
    inverse_root = lax.rsqrt(degree_ref[...])
    current = start_ref[...].T

    for it in range(STEPS):
        ebuf, esend, erecv = emb.at[it], emb_send.at[it], emb_recv.at[it]
        ebuf[span] = (inverse_root * current).astype(jnp.bfloat16)
        acc[...] = jnp.zeros_like(acc)

        def product(d):
            acc[...] += jnp.dot(ebuf[span + d], tiles[span + d], preferred_element_type=jnp.float32)

        exchange(ebuf, esend, erecv, product)
        y_t[...] = inverse_root * acc[...]
        local = lax.dot_general(y_t[...], y_t[...], (((1,), (1,)), ((), ())),
                                precision=lax.Precision.HIGHEST, preferred_element_type=jnp.float32)
        half = width // 2
        quarter = half // 2
        gram[it] = jnp.concatenate([local[0:half], local[half:width]], axis=1)
        own = pl.ds(pl.multiple_of(core * quarter, quarter), quarter)
        its = pl.ds(pl.multiple_of(other * quarter, quarter), quarter)
        first = pltpu.make_async_remote_copy(
            src_ref=gram.at[it, its], dst_ref=gram_near.at[it],
            send_sem=gsend.at[it, 0], recv_sem=grecv.at[it, 0],
            device_id=(group, chip, other), device_id_type=MESH)
        first.start()
        first.wait_recv()
        gram_all[it, chip] = gram[it, own] + gram_near[it]

        def scatter(o):
            to = lax.rem(chip + o, rows_n)
            return pltpu.make_async_remote_copy(
                src_ref=gram_all.at[it, chip], dst_ref=gram_all.at[it, chip],
                send_sem=gall_send.at[it, o], recv_sem=gall_recv.at[it, chip],
                device_id=(group, to, core), device_id_type=MESH)

        def start_one(o, _):
            scatter(o).start()
            return 0

        lax.fori_loop(1, rows_n, start_one, 0)

        def await_one(o, _):
            source = lax.rem(chip + o, rows_n)
            pltpu.make_async_remote_copy(
                src_ref=gram_all.at[it, source], dst_ref=gram_all.at[it, source],
                send_sem=gall_send.at[it, o], recv_sem=gall_recv.at[it, source],
                device_id=(group, source, core), device_id_type=MESH).wait_recv()
            return 0

        lax.fori_loop(1, rows_n, await_one, 0)
        gram_sum[it, own] = jnp.sum(gram_all[it], axis=0)
        last = pltpu.make_async_remote_copy(
            src_ref=gram_sum.at[it, own], dst_ref=gram_sum.at[it, own],
            send_sem=gsend.at[it, 1], recv_sem=grecv.at[it, 1],
            device_id=(group, chip, other), device_id_type=MESH)
        last.start()
        last.wait_recv()
        packed = gram_sum[it] * (1.0 / (blk * total))
        whole = jnp.concatenate([packed[:, 0:width], packed[:, width:2 * width]], axis=0)
        current = jnp.dot(inverse_cholesky(whole), y_t[...],
                          precision=lax.Precision.HIGHEST, preferred_element_type=jnp.float32)
        first.wait_send()
        last.wait_send()

        def sent_one(o, _):
            scatter(o).wait_send()
            return 0

        lax.fori_loop(1, rows_n, sent_one, 0)

    out_ref[...] = current.T
    finish(pts, pts_send, pts_recv)
    for it in range(STEPS):
        finish(emb.at[it], emb_send.at[it], emb_recv.at[it])


def per_device(rows_n, points, start, pair_mask):
    blk, feats = points.shape
    width = start.shape[1]
    span = pair_mask.shape[1]
    slots = 2 * span + 1
    vmem = pl.BlockSpec(memory_space=pltpu.VMEM)
    embedding, degree = pl.pallas_call(
        functools.partial(kernel, rows_n, span),
        out_shape=(jax.ShapeDtypeStruct((blk, width), jnp.float32), jax.ShapeDtypeStruct((1, blk), jnp.float32)),
        in_specs=[vmem, vmem, pl.BlockSpec(memory_space=pltpu.SMEM)],
        out_specs=(vmem, vmem),
        scratch_shapes=[
            pltpu.VMEM((slots, blk + PAD, feats), jnp.int16),
            pltpu.VMEM((4 * feats, blk), jnp.bfloat16),
            pltpu.VMEM((blk, 2 * feats), jnp.bfloat16),
            pltpu.VMEM((slots, blk, blk), jnp.bfloat16),
            pltpu.VMEM((STEPS, slots, width, blk), jnp.bfloat16),
            pltpu.VMEM((width, blk), jnp.float32),
            pltpu.VMEM((width, blk), jnp.float32),
            pltpu.VMEM((STEPS, width // 2, 2 * width), jnp.float32),
            pltpu.VMEM((STEPS, width // 4, 2 * width), jnp.float32),
            pltpu.VMEM((STEPS, rows_n, width // 4, 2 * width), jnp.float32),
            pltpu.VMEM((STEPS, width // 2, 2 * width), jnp.float32),
            pltpu.SemaphoreType.DMA((slots + 1,)),
            pltpu.SemaphoreType.DMA((slots,)),
            pltpu.SemaphoreType.DMA((STEPS, slots + 1)),
            pltpu.SemaphoreType.DMA((STEPS, slots)),
            pltpu.SemaphoreType.DMA((STEPS, 2)),
            pltpu.SemaphoreType.DMA((STEPS, 2)),
            pltpu.SemaphoreType.DMA((STEPS, rows_n)),
            pltpu.SemaphoreType.DMA((STEPS, rows_n)),
        ],
        compiler_params=pltpu.CompilerParams(
            collective_id=0, has_side_effects=True, vmem_limit_bytes=56 * 1024 * 1024),
    )(points, start, pair_mask)
    return embedding, degree[0]


def solution(mesh):
    rows = P(("groups", "row", "col"), None)
    return jax.shard_map(
        functools.partial(per_device, mesh.shape["row"]), mesh=mesh, in_specs=(rows, rows, rows),
        out_specs=(rows, P(("groups", "row", "col"))), check_vma=False)
```
